256 devices in a mesh: dp: 32 (over x_lo, z, core), tp: 8 (over x_hi, y).
Axes of the slice: x: 4 (x_hi: 2, x_lo: 2; x = x_hi * 2 + x_lo), y: 4, z: 8, core: 2. Of those that a mesh axis runs over, the one named last changes fastest.
Arguments:
- queries: bfloat16 [768, 128, 576], P('dp', 'tp'), may hold values from -10 to 10
- new_latent: bfloat16 [768, 576], P('dp'), may hold values from -6 to 6
- hot_cache: bfloat16 [768, 128, 576], P('dp'), may hold values from -6 to 6
- cache_len: int32 [768], P('dp'), may hold values from 1 to 128, 49152 in all
- page_pool: bfloat16 [512, 64, 576], P('dp'), may hold values from -6 to 6
- cold_holder: int32 [768, 4], P('dp'), may hold values from 0 to 31, all different within a row; in each aligned block of 24 rows (0 to 23, 24 to 47, ...) at most 4 rows name the same one
- cold_slot: int32 [768, 4], P('dp'), may hold values from 0 to 15
- residual: bfloat16 [768, 7168], P(None, 'dp'), may hold values from -7 to 7
- value_map: bfloat16 [128, 512, 128], P('tp'), may hold values from -0.25 to 0.25
- out_proj: bfloat16 [16384, 7168], P('tp', 'dp'), may hold values from -0.1875 to 0.1875
- norm_gain: bfloat16 [7168], P('dp'), may hold values from 0.099609375 to 1.8984375
- gate_proj: bfloat16 [7168, 18432], P('dp', 'tp'), may hold values from -0.0625 to 0.0625
- up_proj: bfloat16 [7168, 18432], P('dp', 'tp'), may hold values from -0.0625 to 0.0625
- down_proj: bfloat16 [18432, 7168], P('tp', 'dp'), may hold values from -0.046875 to 0.046875
Outputs:
- layer_out: bfloat16 [768, 7168], P('tp', 'dp')
The draws below stay inside these ranges and needn't reach their ends.
Inputs may be any that keep to these rules, and one draw needn't show every extreme that they name: `cache_len`: at least one request has exactly 128 live rows. `cold_holder`: the 4 cold pages of a request lie on different indices of dp; the 24 requests of one index of dp name one holder at most 4 times, a bound that some block reaches.
All inputs are finite; a program needn't handle non-finite values. No bound on the sum of `cache_len` on one device may be relied on, other than what follows from the above.
Results may differ from the reference program's by a relative error of at most 0.025.
Values may be sent and summed in bfloat16 or wider, within the bound.
No kernel may reach another device: no remote copies, remote signals or barrier semaphores. Data moves between devices by JAX's collectives and lax.ppermute only.
A program may use at most 128 MiB of HBM per device.

```python
import math
import jax
import jax.numpy as jnp
import numpy as np
from jax import lax

D = 7168
H = 128
DC = 512
DR = 64
DV = 128
FF = 18432
PAGE = 64
P_COLD = 4
L_HOT = 128
B_DEV = 24
POOL_DEV = 16
B = 768
KD = 576
CAP = 4
N_DP = 32


def draw_new_latent(key, part):
    key = jax.random.fold_in(key, 11)
    result = jnp.clip(jax.random.normal(key, (B, KD), jnp.float32), -6.0, 6.0)
    return result.astype(jnp.bfloat16)


def draw_queries(key, part):
    key = jax.random.fold_in(key, 12)
    result = jnp.clip(jax.random.normal(key, (B, H, KD), jnp.float32), -6.0, 6.0)
    return result.astype(jnp.bfloat16)


def draw_hot_cache(key, part):
    key = jax.random.fold_in(key, 13)
    result = jnp.clip(jax.random.normal(key, (B, L_HOT, KD), jnp.float32), -6.0, 6.0)
    return result.astype(jnp.bfloat16)


def draw_residual(key, part):
    key = jax.random.fold_in(key, 14)
    first_key = jax.random.fold_in(key, 0)
    column = jnp.arange(D).astype(jnp.float32) / D
    column_scale = 0.4 * 3.0 ** (column / 2.0)
    result = jnp.clip(jax.random.normal(first_key, (B, D), jnp.float32), -6.0, 6.0) * column_scale[None, :]
    return result.astype(jnp.bfloat16)


def with_ends(array, key, low, high):
    index_at = [jax.random.randint(jax.random.fold_in(key, axis), (), 0, length) for axis, length in enumerate(array.shape)]
    longest = array.shape.index(max(array.shape))
    next_to = index_at[:longest] + [(index_at[longest] + 1) % array.shape[longest]] + index_at[longest + 1:]
    return array.at[tuple(index_at)].set(low).at[tuple(next_to)].set(high)


def steps_of(rng, extent, pieces, least, largest):
    factor_of, own = 1.0, jax.random.fold_in(rng, 6)
    for position, blocks in pieces:
        steps = jnp.exp(jax.random.uniform(jax.random.fold_in(own, position), (blocks,), jnp.float32, least / len(pieces), largest / len(pieces)))
        factor_of = factor_of * jnp.repeat(steps, extent[position] // blocks).reshape([-1 if axis == position else 1 for axis in range(len(extent))])
    return factor_of


def profile(count, total, reach, slope):
    weights = [(1 << 20) // math.isqrt(rank ** slope) + 1 for rank in range(2, count + 1)]
    spare, counts = total - reach - (count - 1), [1] * (count - 1)
    while spare > 0:
        movable = [i for i in range(count - 1) if counts[i] < reach]
        mass, left = sum([weights[i] for i in movable]), spare
        for i in movable:
            more = min(reach - counts[i], max(1, left * weights[i] // mass), spare)
            counts[i] = counts[i] + more
            spare = spare - more
    return np.array([reach] + counts)


def ragged_sizes(key, count, total, most, skew):
    if count == 2:
        one = jax.random.randint(key, (), max(1, total - most), min(most, total - 1) + 1)
        return jnp.stack([one, total - one])
    lengths = jnp.asarray(profile(count, total, most, skew), jnp.int32)
    couples = (count - 1) // 2
    donor, sink = lengths[1:1 + 2 * couples:2], lengths[2:2 + 2 * couples:2]
    room = jnp.minimum(donor - 1, most - sink)
    moved = jax.random.randint(jax.random.fold_in(key, 1), (couples,), 0, 1 << 20) % (room + 1)
    lengths = lengths.at[1:1 + 2 * couples:2].set(donor - moved).at[2:2 + 2 * couples:2].set(sink + moved)
    return lengths[jax.random.permutation(jax.random.fold_in(key, 2), count)]


def shared_out(rng, own, number, rows, count, top, limit, skew):
    order = jax.random.permutation(rng, count)
    crowded, common = load_shares(count, rows * top, limit, skew, True), load_shares(count, rows * top, limit, skew, False)
    places = jnp.arange(count)

    def named(lengths, rotation):
        used = int((lengths > 0).sum())
        fixed = max(1, used // 4)
        passed = fixed + (places - fixed + rotation * (used - fixed)) % max(1, count - fixed)
        return jnp.zeros((count,), jnp.int32).at[order[jnp.where(places < fixed, places, passed)]].set(jnp.asarray(lengths, jnp.int32))

    lengths = jnp.where(number % 4 == 0, named(crowded, number // 4), named(common, number - number // 4 - 1))
    mixed = jax.random.permutation(jax.random.fold_in(own, 3), count)
    giver, sink = mixed[0:count // 2 * 2:2], mixed[1:count // 2 * 2:2]
    slack = jnp.minimum(lengths[giver] - 1, limit - lengths[sink]) // 2
    slack = jnp.where((giver == order[0]) | (sink == order[0]) | (lengths[sink] == 0), 0, jnp.maximum(slack, 0))
    passed = jax.random.randint(jax.random.fold_in(own, 4), (count // 2,), 0, 1 << 20) % (slack + 1)
    lengths = lengths.at[giver].add(-passed).at[sink].add(passed)
    members = jnp.searchsorted(jnp.cumsum(lengths), jnp.arange(rows * top), side="right").astype(jnp.int32)
    table = members.reshape(top, rows).T
    table = table[jax.random.permutation(jax.random.fold_in(own, 1), rows)]
    rotation = jax.random.randint(jax.random.fold_in(own, 2), (rows, 1), 0, top)
    return jnp.take_along_axis(table, (jnp.arange(top)[None, :] + rotation) % top, axis=1)


def load_shares(number_of, total, reach, slope, full):
    loads = [(1 << 20) // math.isqrt(rank ** slope) + 1 for rank in range(1, number_of + 1)]
    largest = reach if full else min(reach, max(-(-total // number_of), total * loads[0] // sum(loads)))
    least = 1 if total - largest >= number_of - 1 else 0
    holding, spare = [largest] + [least] * (number_of - 1), total - largest - least * (number_of - 1)
    while spare > 0:
        candidates = [i for i in range(1, number_of) if holding[i] < largest] or [i for i in range(1, number_of) if holding[i] < reach]
        mass, remaining = sum([loads[i] for i in candidates]), spare
        for i in candidates:
            extra = min(reach - holding[i], max(1, remaining * loads[i] // mass), spare)
            holding[i] = holding[i] + extra
            spare = spare - extra
    return np.array(holding)


def normal_values(stream_key, dims, deviation, most, cuts=(), kind=jnp.bfloat16):
    loudness = steps_of(stream_key, dims, cuts, -0.22, 0.18) if cuts else 1.0
    array = jax.random.normal(stream_key, dims, jnp.float32) * deviation * loudness
    return jnp.minimum(jnp.maximum(array, -most), most).astype(kind)


def setup_inputs(seed: int = 0) -> dict:
    key_list = jax.random.split(jax.random.key(seed), 15)
    queries = draw_queries(jax.random.fold_in(key_list[14], 71), 0)
    new_latent = draw_new_latent(jax.random.fold_in(key_list[14], 71), 0)
    hot_cache = draw_hot_cache(jax.random.fold_in(key_list[14], 71), 0)
    cache_len = ragged_sizes(key_list[3], B, B * L_HOT // 2, L_HOT, 2).astype(jnp.int32)
    page_pool = normal_values(key_list[4], (N_DP * POOL_DEV, PAGE, KD), 1.0, 6.0, ((0, 32),))
    cold_holder_keys = jax.random.split(jax.random.fold_in(key_list[5], 1), B // B_DEV)
    cold_holder_turns = jax.random.permutation(jax.random.fold_in(key_list[5], 3), B // B_DEV)
    cold_holder = jax.vmap(lambda own, number: shared_out(jax.random.fold_in(key_list[5], 2), own, number, B_DEV, N_DP, P_COLD, CAP, 2))(cold_holder_keys, cold_holder_turns).reshape((B, P_COLD))
    cold_slot = with_ends(jax.random.randint(key_list[6], (B, P_COLD), 0, POOL_DEV), jax.random.fold_in(key_list[6], 1), 0, POOL_DEV - 1).astype(jnp.int32)
    residual = draw_residual(jax.random.fold_in(key_list[14], 71), 0)
    value_map = normal_values(key_list[8], (H, DC, DV), DC ** -0.5, 0.25, ((0, 8),))
    out_proj = normal_values(key_list[9], (H * DV, D), (DV * 8) ** -0.5, 0.1875, ((0, 8), (1, 32)))
    norm_gain = jnp.clip(1.0 + 0.18 * jax.random.normal(key_list[10], (D,), jnp.float32), 0.099609375, 1.8984375).astype(jnp.bfloat16)
    gate_proj = normal_values(key_list[11], (D, FF), D ** -0.5, 0.0625, ((0, 32), (1, 8)))
    up_proj = normal_values(key_list[12], (D, FF), D ** -0.5, 0.0625, ((0, 32), (1, 8)))
    down_proj = normal_values(key_list[13], (FF, D), FF ** -0.5, 0.046875, ((0, 8), (1, 32)))
    return dict(queries=queries, new_latent=new_latent, hot_cache=hot_cache, cache_len=cache_len, page_pool=page_pool, cold_holder=cold_holder, cold_slot=cold_slot, residual=residual, value_map=value_map, out_proj=out_proj, norm_gain=norm_gain, gate_proj=gate_proj, up_proj=up_proj, down_proj=down_proj)


def attend(query_rows, latent_rows, hot_rows, live_counts, cold_rows):
    all_keys = jnp.concatenate([cold_rows, hot_rows, latent_rows[:, None, :]], axis=1)
    count = query_rows.shape[0]
    positions = jnp.arange(L_HOT)
    hot_live = positions[None, :] < live_counts[:, None]
    is_live = jnp.concatenate([jnp.ones((count, cold_rows.shape[1]), bool), hot_live, jnp.ones((count, 1), bool)], axis=1)
    score_scale = (DV + DR) ** (-0.5)
    scores = jnp.einsum('bhk,bnk->bhn', query_rows.astype(jnp.float32), all_keys.astype(jnp.float32)) * score_scale
    scores = jnp.where(is_live[:, None, :], scores, -1e+30)
    highest = lax.optimization_barrier(jnp.max(scores, axis=-1, keepdims=True))
    expo = jnp.exp(scores - highest)
    weights = (expo / lax.optimization_barrier(jnp.sum(expo, axis=-1, keepdims=True))).astype(jnp.bfloat16)
    latent_out = jnp.einsum('bhn,bnc->bhc', weights.astype(jnp.float32), all_keys[:, :, :DC].astype(jnp.float32))
    return latent_out.astype(jnp.bfloat16)

def reference(queries, new_latent, hot_cache, cache_len, page_pool, cold_holder, cold_slot, residual, value_map, out_proj, norm_gain, gate_proj, up_proj, down_proj):
    page_ids = (cold_holder * POOL_DEV + cold_slot).astype(jnp.int32)

    def owner_block(inputs):
        query_rows, latent_rows, hot_rows, live_counts, id_rows = inputs
        cold_rows = page_pool[id_rows].reshape(B_DEV, P_COLD * PAGE, KD)
        return attend(query_rows, latent_rows, hot_rows, live_counts, cold_rows)
    latent_out = lax.map(owner_block, (queries.reshape(N_DP, B_DEV, H, KD), new_latent.reshape(N_DP, B_DEV, KD), hot_cache.reshape(N_DP, B_DEV, L_HOT, KD), cache_len.reshape(N_DP, B_DEV), page_ids.reshape(N_DP, B_DEV, P_COLD))).reshape(B, H, DC)
    head_out = jnp.einsum('bhc,hcv->bhv', latent_out.astype(jnp.float32), value_map.astype(jnp.float32))
    head_out = head_out.astype(jnp.bfloat16).reshape(B, H * DV)
    hidden = residual.astype(jnp.float32) + jnp.dot(head_out, out_proj, preferred_element_type=jnp.float32)
    inverse = lax.rsqrt(lax.optimization_barrier(jnp.mean(hidden * hidden, axis=-1, keepdims=True)) + 1e-06)
    normed = (hidden * inverse * norm_gain.astype(jnp.float32)).astype(jnp.bfloat16)
    both_proj = jnp.concatenate([gate_proj, up_proj], axis=1)
    block_width = D // N_DP

    def accumulate(carry, block_index):
        normed_block = lax.dynamic_slice_in_dim(normed, block_index * block_width, block_width, 1)
        proj_block = lax.dynamic_slice_in_dim(both_proj, block_index * block_width, block_width, 0)
        product = jnp.dot(normed_block, proj_block, preferred_element_type=jnp.float32)
        product = lax.optimization_barrier(product.astype(jnp.bfloat16)).astype(jnp.float32)
        return (carry + product, None)
    gate_up, _ = lax.scan(accumulate, jnp.zeros((B, 2 * FF), jnp.float32), jnp.arange(N_DP, dtype=jnp.int32))
    activated = (jax.nn.silu(gate_up[:, :FF]) * gate_up[:, FF:]).astype(jnp.bfloat16)
    layer_out = hidden + jnp.dot(activated, down_proj, preferred_element_type=jnp.float32)
    return layer_out.astype(jnp.bfloat16)
```

```python
import jax
import jax.numpy as jnp
from jax import lax
from jax.experimental import pallas as pl
from jax.experimental.pallas import tpu as pltpu
from jax.sharding import Mesh
from jax.sharding import PartitionSpec as P

DC = 512
DR = 64
DV = 128
NZ = 8
DP = ("xlo", "z", "core")
TP = ("xhi", "y")
BF = jnp.bfloat16
F32 = jnp.float32


def dot(a, b):
    return jnp.dot(a, b, preferred_element_type=F32)


def attend_kernel(len_ref, q_ref, cold_ref, hot_ref, new_ref, out_ref):
    scale = (DV + DR) ** (-0.5)
    heads = q_ref.shape[1] * q_ref.shape[0]
    q = q_ref[...].reshape(heads, q_ref.shape[-1])
    cold = cold_ref[0]
    hot = hot_ref[0]
    new = new_ref[0]
    nt = (((1,), (1,)), ((), ()))
    s_cold = lax.dot_general(q, cold, nt, preferred_element_type=F32) * scale
    s_hot = lax.dot_general(q, hot, nt, preferred_element_type=F32) * scale
    live = lax.broadcasted_iota(jnp.int32, s_hot.shape, 1) < len_ref[pl.program_id(0)]
    s_hot = jnp.where(live, s_hot, -1e30)
    s_new = jnp.sum(q.astype(F32) * new.astype(F32), axis=1, keepdims=True) * scale
    top = jnp.maximum(jnp.max(s_cold, axis=1, keepdims=True), jnp.max(s_hot, axis=1, keepdims=True))
    top = jnp.maximum(top, s_new)
    e_cold = jnp.exp(s_cold - top)
    e_hot = jnp.exp(s_hot - top)
    e_new = jnp.exp(s_new - top)
    total = jnp.sum(e_cold, axis=1, keepdims=True) + jnp.sum(e_hot, axis=1, keepdims=True) + e_new
    w_cold = (e_cold / total).astype(BF)
    w_hot = (e_hot / total).astype(BF)
    w_new = (e_new / total).astype(BF).astype(F32)
    out = dot(w_cold, cold[:, :DC]) + dot(w_hot, hot[:, :DC])
    out = out + w_new * new[:, :DC].astype(F32)
    out_ref[...] = out.astype(BF).reshape(out_ref.shape)


def attend(q, cold, hot, new, lens):
    groups, rows, heads, width = q.shape
    return pl.pallas_call(
        attend_kernel,
        grid=(rows,),
        in_specs=[
            pl.BlockSpec(memory_space=pltpu.SMEM),
            pl.BlockSpec((groups, None, heads, width), lambda r: (0, r, 0, 0)),
            pl.BlockSpec((1,) + cold.shape[1:], lambda r: (r, 0, 0)),
            pl.BlockSpec((1,) + hot.shape[1:], lambda r: (r, 0, 0)),
            pl.BlockSpec((1, 1, width), lambda r: (r, 0, 0)),
        ],
        out_specs=pl.BlockSpec((groups, None, heads, DC), lambda r: (0, r, 0, 0)),
        out_shape=jax.ShapeDtypeStruct((groups, rows, heads, DC), BF),
        compiler_params=pltpu.CompilerParams(vmem_limit_bytes=32 << 20),
    )(lens, q, cold, hot, new[:, None, :])


UP = [(i, (i + 1) % NZ) for i in range(NZ)]
DOWN = [(i, (i - 1) % NZ) for i in range(NZ)]
SWAP = [(0, 1), (1, 0)]


def paired(x, axis):
    other = lax.ppermute(x, axis, SWAP)
    first = lax.axis_index(axis) == 0
    return jnp.where(first, x, other), jnp.where(first, other, x)


def gather_dot(x, w):
    rows = x.shape[0]
    a, b = paired(x, "xlo")
    mine = jnp.stack([a, b])
    blocks = [None] * NZ
    blocks[0] = mine
    up = down = mine
    for k in range(1, 4):
        up = lax.ppermute(up, "z", UP)
        down = lax.ppermute(down, "z", DOWN)
        blocks[NZ - k] = up
        blocks[k] = down
    far = lax.ppermute(up[0], "z", UP), lax.ppermute(down[1], "z", DOWN)
    blocks[4] = jnp.stack(far)
    outs = []
    for blk in blocks:
        other = lax.ppermute(blk, "core", SWAP)
        both = jnp.concatenate([blk, other]).reshape(4 * rows, -1)
        outs.append(dot(both, w).astype(BF))
    y = jnp.stack(outs + outs[:-1]).reshape(2 * NZ - 1, 2, 2, rows, -1)
    z = lax.axis_index("z")
    y = lax.dynamic_slice_in_dim(y, (NZ - z) % NZ, NZ, 0)
    core0 = lax.axis_index("core") == 0
    c0 = jnp.where(core0, y[:, 0], y[:, 1])
    c1 = jnp.where(core0, y[:, 1], y[:, 0])
    y = jnp.stack([c0, c1], axis=2)
    return y.transpose(1, 0, 2, 3, 4).reshape(4 * NZ * rows, -1)


def scatter_rows(x, axes):
    n = lax.axis_size(axes)
    parts = lax.all_to_all(x.reshape(n, x.shape[0] // n, -1), axes, 0, 0, tiled=True)
    return jnp.sum(parts.astype(F32), axis=0)


def on_device(
    queries,
    new_latent,
    hot_cache,
    cache_len,
    page_pool,
    cold_holder,
    cold_slot,
    residual,
    value_map,
    out_proj,
    norm_gain,
    gate_proj,
    up_proj,
    down_proj,
):
    owners = lax.axis_size(DP)
    shares = lax.axis_size(TP)
    share = lax.axis_index(TP)
    rows_dev, pages_each = cold_holder.shape
    rows_own = rows_dev // shares
    capacity = (rows_dev * pages_each + owners - 1) // owners + 1
    width = queries.shape[-1]

    q_rows = lax.all_to_all(
        queries.reshape(shares, rows_own, queries.shape[1], width), TP, 0, 0, tiled=True
    )

    holder = cold_holder.reshape(-1)
    slot_ids = cold_slot.reshape(-1)
    count = holder.shape[0]
    place = jnp.arange(count, dtype=jnp.int32)
    same = (holder[:, None] == holder[None, :]) & (place[None, :] < place[:, None])
    rank = jnp.sum(same.astype(jnp.int32), axis=1)
    seat = holder * capacity + rank
    seats = jnp.arange(owners * capacity, dtype=jnp.int32)
    wanted = jnp.sum(jnp.where(seats[:, None] == seat[None, :], slot_ids[None, :], 0), axis=1)
    wanted = lax.all_to_all(wanted.reshape(owners, capacity), DP, 0, 0, tiled=True)

    page_share = page_pool.shape[1] // shares
    pool = lax.dynamic_slice_in_dim(page_pool, share * page_share, page_share, 1)
    sent = pool[wanted.reshape(-1)].reshape(owners, capacity * page_share, width)
    fetched = lax.all_to_all(sent, DP, 0, 0, tiled=True)
    fetched = fetched.reshape(owners * capacity, page_share, width)[seat]
    cold = lax.all_to_all(
        fetched.reshape(shares, rows_own * pages_each * page_share, width), TP, 0, 0, tiled=True
    )
    cold = cold.reshape(shares, rows_own, pages_each * page_share, width).transpose(1, 0, 2, 3)
    cold = cold.reshape(rows_own, -1, width)

    start = share * rows_own
    hot = lax.dynamic_slice_in_dim(hot_cache, start, rows_own, 0)
    new = lax.dynamic_slice_in_dim(new_latent, start, rows_own, 0)
    lens = lax.dynamic_slice_in_dim(cache_len, start, rows_own, 0)
    latent = attend(q_rows, cold, hot, new, lens)
    latent = lax.all_to_all(latent, TP, 0, 0, tiled=True)
    latent = latent.reshape(rows_dev, -1, DC)
    head_rows = jnp.einsum("bhc,hcv->bhv", latent, value_map, preferred_element_type=F32)
    head_rows = head_rows.astype(BF).reshape(rows_dev, -1)

    attended = scatter_rows(gather_dot(head_rows, out_proj), TP)
    row_count = attended.shape[0]
    res = lax.dynamic_slice_in_dim(residual, share * row_count, row_count, 0)
    hidden = res.astype(F32) + attended

    squares = jnp.sum(hidden * hidden, axis=1, keepdims=True)
    high = squares.astype(BF)
    low = (squares - high.astype(F32)).astype(BF)
    scaled = (hidden * norm_gain.astype(F32)[None, :]).astype(BF)
    cols = scaled.shape[1]
    packed = jnp.concatenate(
        [scaled, high, low, jnp.zeros((row_count, 30), BF)], axis=1
    )
    packed = jnp.broadcast_to(packed[None], (shares,) + packed.shape)
    packed = lax.all_to_all(packed, TP, 0, 0, tiled=True).reshape(-1, packed.shape[-1])
    scaled = packed[:, :cols]
    squares = packed[:, cols].astype(F32) + packed[:, cols + 1].astype(F32)
    sums = lax.all_to_all(squares.reshape(owners, rows_dev), DP, 0, 0, tiled=True)
    full_width = cols * owners
    inverse = lax.rsqrt(jnp.sum(sums, axis=0) / full_width + 1e-06)

    both_proj = jnp.concatenate([gate_proj, up_proj], axis=1)
    z = lax.axis_index("z")
    core = lax.axis_index("core")
    by_place = scaled.reshape(2, NZ, 2, rows_dev, cols)

    def part(k, xs):
        x = lax.dynamic_slice_in_dim(by_place, (z + k) % NZ, 1, 1)[xs, 0]
        mine = lax.dynamic_slice_in_dim(x, core, 1, 1).reshape(-1, cols)
        theirs = lax.dynamic_slice_in_dim(x, 1 - core, 1, 1).reshape(-1, cols)
        away = lax.ppermute(dot(theirs, both_proj).astype(BF), "core", SWAP)
        return dot(mine, both_proj).astype(BF).astype(F32) + away.astype(F32)

    first, second, every = slice(0, 1), slice(1, 2), slice(0, 2)
    up = lax.ppermute(part(4, first).astype(BF), "z", UP).astype(F32)
    down = lax.ppermute(part(4, second).astype(BF), "z", DOWN).astype(F32)
    none = jnp.zeros_like(up)
    up = jnp.concatenate([up, none])
    down = jnp.concatenate([none, down])
    for k in (3, 2, 1):
        up = lax.ppermute((part(k, every) + up).astype(BF), "z", UP).astype(F32)
        down = lax.ppermute((part(NZ - k, every) + down).astype(BF), "z", DOWN).astype(F32)
    total = (part(0, every) + up + down).reshape(2, rows_dev, -1)
    xlo0 = lax.axis_index("xlo") == 0
    keep = jnp.where(xlo0, total[0], total[1])
    give = jnp.where(xlo0, total[1], total[0])
    gate_up = keep + lax.ppermute(give.astype(BF), "xlo", SWAP).astype(F32)
    gate_up = gate_up * inverse[:, None]
    hidden_cols = gate_proj.shape[1]
    activated = (jax.nn.silu(gate_up[:, :hidden_cols]) * gate_up[:, hidden_cols:]).astype(BF)

    summed = scatter_rows(gather_dot(activated, down_proj), TP)
    return (hidden + summed).astype(BF)


def solution(mesh):
    grid = Mesh(mesh.devices.reshape(2, NZ, 2, 2, 4), DP + TP)
    placed = (
        P(DP, TP, None),
        P(DP, None),
        P(DP, None, None),
        P(DP),
        P(DP, None, None),
        P(DP, None),
        P(DP, None),
        P(None, DP),
        P(TP, None, None),
        P(TP, DP),
        P(DP),
        P(DP, TP),
        P(DP, TP),
        P(TP, DP),
    )
    return jax.shard_map(
        on_device, mesh=grid, in_specs=placed, out_specs=P(TP, DP), check_vma=False
    )
```

```python
import jax
import jax.numpy as jnp
from jax import lax
from jax.experimental import pallas as pl
from jax.experimental.pallas import tpu as pltpu
from jax.sharding import Mesh
from jax.sharding import PartitionSpec as P

DC = 512
DR = 64
DV = 128
NZ = 8
DP = ("xlo", "z", "core")
TP = ("xhi", "y")
BF = jnp.bfloat16
F32 = jnp.float32


def dot(a, b):
    return jnp.dot(a, b, preferred_element_type=F32)


def attend_kernel(start_ref, len_ref, q_ref, cold_ref, hot_ref, new_ref, out_ref):
    scale = (DV + DR) ** (-0.5)
    heads = q_ref.shape[1] * q_ref.shape[0]
    width = q_ref.shape[-1]
    q = q_ref[...].reshape(heads, width)
    cold = cold_ref[...].reshape(-1, width)
    hot = hot_ref[0]
    new = new_ref[0]
    nt = (((1,), (1,)), ((), ()))
    s_cold = lax.dot_general(q, cold, nt, preferred_element_type=F32) * scale
    s_hot = lax.dot_general(q, hot, nt, preferred_element_type=F32) * scale
    live = lax.broadcasted_iota(jnp.int32, s_hot.shape, 1) < len_ref[start_ref[0] + pl.program_id(0)]
    s_hot = jnp.where(live, s_hot, -1e30)
    s_new = jnp.sum(q.astype(F32) * new.astype(F32), axis=1, keepdims=True) * scale
    top = jnp.maximum(jnp.max(s_cold, axis=1, keepdims=True), jnp.max(s_hot, axis=1, keepdims=True))
    top = jnp.maximum(top, s_new)
    e_cold = jnp.exp(s_cold - top)
    e_hot = jnp.exp(s_hot - top)
    e_new = jnp.exp(s_new - top)
    total = jnp.sum(e_cold, axis=1, keepdims=True) + jnp.sum(e_hot, axis=1, keepdims=True) + e_new
    w_cold = (e_cold / total).astype(BF)
    w_hot = (e_hot / total).astype(BF)
    w_new = (e_new / total).astype(BF).astype(F32)
    out = dot(w_cold, cold[:, :DC]) + dot(w_hot, hot[:, :DC])
    out = out + w_new * new[:, :DC].astype(F32)
    out_ref[...] = out.astype(BF).reshape(out_ref.shape)


def attend(start, lens, q, cold, hot, new):
    groups, rows, heads, width = q.shape
    return pl.pallas_call(
        attend_kernel,
        grid_spec=pltpu.PrefetchScalarGridSpec(
            num_scalar_prefetch=2,
            grid=(rows,),
            in_specs=[
                pl.BlockSpec((groups, None, heads, width), lambda r, s, n: (0, r, 0, 0)),
                pl.BlockSpec((groups, None) + cold.shape[2:], lambda r, s, n: (0, r, 0, 0)),
                pl.BlockSpec((1,) + hot.shape[1:], lambda r, s, n: (s[0] + r, 0, 0)),
                pl.BlockSpec((1, 1, width), lambda r, s, n: (s[0] + r, 0, 0)),
            ],
            out_specs=pl.BlockSpec((groups, None, heads, DC), lambda r, s, n: (0, r, 0, 0)),
        ),
        out_shape=jax.ShapeDtypeStruct((groups, rows, heads, DC), BF),
        compiler_params=pltpu.CompilerParams(vmem_limit_bytes=32 << 20),
    )(start, lens, q, cold, hot, new[:, None, :])


UP = [(i, (i + 1) % NZ) for i in range(NZ)]
DOWN = [(i, (i - 1) % NZ) for i in range(NZ)]
SWAP = [(0, 1), (1, 0)]
APART = [(2 * i, 2 * ((i + 1) % NZ)) for i in range(NZ)]
APART += [(2 * i + 1, 2 * ((i - 1) % NZ) + 1) for i in range(NZ)]


def swap(x, axis):
    return lax.ppermute(x, axis, SWAP)


def first(axis):
    return lax.axis_index(axis) == 0


def ordered(mine, other, axis):
    f = first(axis)
    return jnp.stack([jnp.where(f, mine, other), jnp.where(f, other, mine)])


def divide(x, axis, dim):
    n = x.shape[dim] // 2
    low = lax.slice_in_dim(x, 0, n, axis=dim)
    high = lax.slice_in_dim(x, n, 2 * n, axis=dim)
    f = first(axis)
    return jnp.where(f, low, high), jnp.where(f, high, low)


def requarter(w, dim):
    keep, give = divide(w, "xlo", dim)
    w = jnp.stack([keep, swap(give, "xlo")])
    keep, give = divide(w, "core", dim + 1)
    return jnp.stack([keep, swap(give, "core")], axis=1)


def gather_quarter(x):
    x = jnp.stack([x, swap(x, "core")])
    return jnp.stack([x, swap(x, "xlo")])


def gather_z(x, dim):
    z = lax.axis_index("z")
    x = jnp.expand_dims(x, dim)
    shape = list(x.shape)
    shape[dim] = NZ
    n = x.shape[0] // 2

    def put(all_x, block, k, row=0):
        at = [row] + [0] * (x.ndim - 1)
        at[dim] = (at[dim] if dim else 0) + (z + k) % NZ
        return lax.dynamic_update_slice(all_x, block, at)

    out = put(jnp.zeros(shape, x.dtype), x, 0)
    up = down = x
    for k in range(1, 4):
        up = lax.ppermute(up, "z", UP)
        down = lax.ppermute(down, "z", DOWN)
        out = put(put(out, up, NZ - k), down, k)
    half = x.shape[1 - dim if dim < 2 else 0] // 2
    axis = 1 - dim if dim < 2 else 0
    up = lax.ppermute(lax.slice_in_dim(up, 0, half, axis=axis), "z", UP)
    down = lax.ppermute(lax.slice_in_dim(down, half, 2 * half, axis=axis), "z", DOWN)
    return put(out, jnp.concatenate([up, down], axis=axis), 4)


def gather_pool(pool):
    z = lax.axis_index("z")
    f = first("core")
    x = ordered(pool, swap(pool, "xlo"), "xlo")
    x = ordered(x, swap(x, "core"), "core")[:, None]
    out = jnp.zeros((2, NZ) + x.shape[2:], x.dtype)

    def put(out, block, k, core=0):
        return lax.dynamic_update_slice(out, block, [core, (z + k) % NZ] + [0] * (x.ndim - 2))

    out = put(out, x, 0)
    away = jnp.where(f, NZ - 1, 1)
    block = x
    for k in range(1, 4):
        block = lax.ppermute(block, ("z", "core"), APART)
        other = swap(block, "core")
        out = put(put(out, block, k * away), other, -k * away + NZ * 4)
    half = jnp.where(f, block[:1], block[1:])
    half = lax.ppermute(half, ("z", "core"), APART)
    return put(out, ordered(half[0], swap(half, "core")[0], "core"), 4)


def dots(x, w):
    tp = lax.axis_size(TP)
    w = w.reshape((4,) + w.shape[2:])
    y = jnp.stack([dot(x, w[j]).astype(BF).reshape(tp, -1, w.shape[-1]) for j in range(4)], axis=1)
    return y.reshape((tp, 2, 2) + y.shape[2:])


def sum_tp(y):
    return jnp.sum(lax.all_to_all(y, TP, 0, 0, tiled=True).astype(F32), axis=0)


def on_device(
    queries,
    new_latent,
    hot_cache,
    cache_len,
    page_pool,
    cold_holder,
    cold_slot,
    residual,
    value_map,
    out_proj,
    norm_gain,
    gate_proj,
    up_proj,
    down_proj,
):
    shares = lax.axis_size(TP)
    share = lax.axis_index(TP)
    z = lax.axis_index("z")
    rows_dev, pages_each = cold_holder.shape
    rows_own = rows_dev // shares
    width = queries.shape[-1]
    slots = page_pool.shape[0]

    page_share = page_pool.shape[1] // shares
    pool = lax.dynamic_slice_in_dim(page_pool, share * page_share, page_share, 1)
    pages = gather_pool(pool).reshape(-1, page_share, width)

    q_rows = lax.all_to_all(
        queries.reshape(shares, rows_own, queries.shape[1], width), TP, 0, 0, tiled=True
    )

    holder = cold_holder.reshape(-1)
    order = (holder % 2) * NZ * 2 + (holder // 2 % NZ) * 2 + holder // (2 * NZ)
    fetched = pages[order * slots + cold_slot.reshape(-1)]
    fetched = fetched.reshape(shares, rows_own, pages_each * page_share, width)
    fetched, q_rows = lax.optimization_barrier((fetched, q_rows))
    cold = lax.all_to_all(fetched, TP, 0, 0, tiled=True)

    start = (share * rows_own).reshape(1)
    latent = attend(start, cache_len, q_rows, cold, hot_cache, new_latent)
    latent = lax.all_to_all(latent, TP, 0, 0, tiled=True)
    latent = latent.reshape(rows_dev, -1, DC)
    head_rows = jnp.einsum("bhc,hcv->bhv", latent, value_map, preferred_element_type=F32)
    head_rows = head_rows.astype(BF).reshape(rows_dev, 2, 2, -1).transpose(1, 2, 0, 3)

    w_out = requarter(out_proj, 0)
    w_down = requarter(down_proj, 0)
    w_both = requarter(jnp.stack([gate_proj, up_proj]), 2)
    cols, units = w_both.shape[3:]
    lanes = -(-units // 128) * 128
    deep = 256
    w_both = jnp.pad(w_both, [(0, 0)] * 3 + [(0, deep - cols), (0, lanes - units)])
    w_both = w_both.transpose(0, 1, 3, 2, 4).reshape(4, deep, 2 * lanes)
    row_id = lax.broadcasted_iota(jnp.int32, w_both.shape, 1)
    col_id = lax.broadcasted_iota(jnp.int32, w_both.shape, 2)
    piece = lax.broadcasted_iota(jnp.int32, w_both.shape, 0)
    passed = (piece == 0) & (row_id >= cols) & (row_id < cols + 2) & (col_id - units == row_id - cols)
    w_both = jnp.where(passed, jnp.ones((), BF), w_both)

    row_count = residual.shape[0] // shares
    res = lax.dynamic_slice_in_dim(residual, share * row_count, row_count, 0)
    gain = jnp.broadcast_to(norm_gain[None], (16, cols))
    res = gather_quarter(jnp.concatenate([res, gain]))
    res, gain = res[:, :, :row_count], res[:, :, row_count : row_count + 1]

    keep = jnp.where(first("core"), head_rows[:, 0], head_rows[:, 1])
    give = jnp.where(first("core"), head_rows[:, 1], head_rows[:, 0])
    mine = ordered(keep, swap(give, "core"), "core")
    keep = jnp.where(first("xlo"), mine[:, 0], mine[:, 1])
    give = jnp.where(first("xlo"), mine[:, 1], mine[:, 0])
    mine = ordered(keep, swap(give, "xlo"), "xlo")
    heads = gather_z(mine, 1).reshape(residual.shape[0], -1)

    attended = sum_tp(dots(heads, w_out))
    attended = attended + swap(attended.astype(BF), "core")[:, ::-1].astype(F32)
    attended = attended + swap(attended.astype(BF), "xlo")[::-1].astype(F32)
    hidden = res.astype(F32) + attended

    squares = jnp.sum(hidden * hidden, axis=(0, 1, 3))[:, None]
    high = squares.astype(BF)
    low = (squares - high.astype(F32)).astype(BF)
    scaled = (hidden * gain.astype(F32)).astype(BF).reshape(4, row_count, cols)
    extra = jnp.concatenate([high, low, jnp.zeros((row_count, deep - cols - 2), BF)], axis=1)
    extra = jnp.stack([extra] + [jnp.zeros_like(extra)] * 3)
    scaled = jnp.concatenate([scaled, extra], axis=2)
    scaled = jnp.broadcast_to(scaled[None], (shares,) + scaled.shape)
    scaled = lax.all_to_all(scaled, TP, 0, 0, tiled=True)

    def part(k):
        x = lax.dynamic_index_in_dim(scaled, (z + k) % NZ, 0, keepdims=False)
        x = x.transpose(1, 0, 2).reshape(row_count, -1)
        return dot(x, w_both.reshape(4 * deep, -1))

    far = part(4)
    half = row_count // 2
    up = lax.ppermute(far[:half].astype(BF), "z", UP).astype(F32)
    down = lax.ppermute(far[half:].astype(BF), "z", DOWN).astype(F32)
    none = jnp.zeros_like(up)
    up = jnp.concatenate([up, none])
    down = jnp.concatenate([none, down])
    for k in (3, 2, 1):
        up = lax.ppermute((part(k) + up).astype(BF), "z", UP).astype(F32)
        down = lax.ppermute((part(NZ - k) + down).astype(BF), "z", DOWN).astype(F32)
    total = part(0) + up + down
    sums = total[:, units : units + 1] + total[:, units + 1 : units + 2]
    inverse = lax.rsqrt(sums / (4 * NZ * cols) + 1e-06)
    gate = total[:, :units] * inverse
    activated = (jax.nn.silu(gate) * (total[:, lanes : lanes + units] * inverse)).astype(BF)

    activated = gather_z(activated, 0).reshape(residual.shape[0], -1)
    summed = sum_tp(dots(activated, w_down))
    summed = summed[:, 0] + swap(summed[:, 1].astype(BF), "core").astype(F32)
    summed = summed[0] + swap(summed[1].astype(BF), "xlo").astype(F32)
    return (hidden[0, 0] + summed).astype(BF)


def solution(mesh):
    grid = Mesh(mesh.devices.reshape(2, NZ, 2, 2, 4), DP + TP)
    placed = (
        P(DP, TP, None),
        P(DP, None),
        P(DP, None, None),
        P(DP),
        P(DP, None, None),
        P(DP, None),
        P(DP, None),
        P(None, DP),
        P(TP, None, None),
        P(TP, DP),
        P(DP),
        P(DP, TP),
        P(DP, TP),
        P(TP, DP),
    )
    return jax.shard_map(
        on_device, mesh=grid, in_specs=placed, out_specs=P(TP, DP), check_vma=False
    )
```

```python
import jax
import jax.numpy as jnp
from jax import lax
from jax.experimental import pallas as pl
from jax.experimental.pallas import tpu as pltpu
from jax.sharding import Mesh
from jax.sharding import PartitionSpec as P

DC = 512
DR = 64
DV = 128
NZ = 8
DP = ("xlo", "z", "core")
TP = ("xhi", "y")
BF = jnp.bfloat16
F32 = jnp.float32


def dot(a, b):
    return jnp.dot(a, b, preferred_element_type=F32)


def attend_kernel(len_ref, q_ref, cold_ref, hot_ref, new_ref, out_ref):
    scale = (DV + DR) ** (-0.5)
    heads = q_ref.shape[1] * q_ref.shape[0]
    width = q_ref.shape[-1]
    q = q_ref[...].reshape(heads, width)
    side = -(-width // 128) * 128
    cold = cold_ref[0]
    cold = [cold[:, at : at + width] for at in range(0, cold.shape[1], side)]
    cold = jnp.concatenate(cold, axis=0)
    hot = hot_ref[0]
    new = new_ref[0]
    nt = (((1,), (1,)), ((), ()))
    s_cold = lax.dot_general(q, cold, nt, preferred_element_type=F32) * scale
    s_hot = lax.dot_general(q, hot, nt, preferred_element_type=F32) * scale
    live = lax.broadcasted_iota(jnp.int32, s_hot.shape, 1) < len_ref[pl.program_id(0)]
    s_hot = jnp.where(live, s_hot, -1e30)
    s_new = jnp.sum(q.astype(F32) * new.astype(F32), axis=1, keepdims=True) * scale
    top = jnp.maximum(jnp.max(s_cold, axis=1, keepdims=True), jnp.max(s_hot, axis=1, keepdims=True))
    top = jnp.maximum(top, s_new)
    e_cold = jnp.exp(s_cold - top)
    e_hot = jnp.exp(s_hot - top)
    e_new = jnp.exp(s_new - top)
    total = jnp.sum(e_cold, axis=1, keepdims=True) + jnp.sum(e_hot, axis=1, keepdims=True) + e_new
    w_cold = (e_cold / total).astype(BF)
    w_hot = (e_hot / total).astype(BF)
    w_new = (e_new / total).astype(BF).astype(F32)
    out = dot(w_cold, cold[:, :DC]) + dot(w_hot, hot[:, :DC])
    out = out + w_new * new[:, :DC].astype(F32)
    out_ref[...] = out.astype(BF).reshape(out_ref.shape)


def attend(lens, q, cold, hot, new):
    groups, rows, heads, width = q.shape
    return pl.pallas_call(
        attend_kernel,
        grid_spec=pltpu.PrefetchScalarGridSpec(
            num_scalar_prefetch=1,
            grid=(rows,),
            in_specs=[
                pl.BlockSpec((groups, None, heads, width), lambda r, n: (0, r, 0, 0)),
                pl.BlockSpec((1,) + cold.shape[1:], lambda r, n: (r, 0, 0)),
                pl.BlockSpec((1,) + hot.shape[1:], lambda r, n: (r, 0, 0)),
                pl.BlockSpec((1, 1, width), lambda r, n: (r, 0, 0)),
            ],
            out_specs=pl.BlockSpec((groups, None, heads, DC), lambda r, n: (0, r, 0, 0)),
        ),
        out_shape=jax.ShapeDtypeStruct((groups, rows, heads, DC), BF),
        compiler_params=pltpu.CompilerParams(vmem_limit_bytes=12 << 20),
    )(lens, q, cold, hot, new[:, None, :])


UP = [(i, (i + 1) % NZ) for i in range(NZ)]
DOWN = [(i, (i - 1) % NZ) for i in range(NZ)]
SWAP = [(0, 1), (1, 0)]


def swap(x, axis):
    return lax.ppermute(x, axis, SWAP)


def first(axis):
    return lax.axis_index(axis) == 0


def ordered(mine, other, axis):
    f = first(axis)
    return jnp.stack([jnp.where(f, mine, other), jnp.where(f, other, mine)])


def divide(x, axis, dim):
    n = x.shape[dim] // 2
    low = lax.slice_in_dim(x, 0, n, axis=dim)
    high = lax.slice_in_dim(x, n, 2 * n, axis=dim)
    f = first(axis)
    return jnp.where(f, low, high), jnp.where(f, high, low)


def after(x, y):
    return lax.optimization_barrier((x, y))[0]


def both_ways(up, down, beside=()):
    beside = [(after(x, down), axis) for x, axis in beside]
    step = lax.ppermute(up, "z", UP), lax.ppermute(down, "z", DOWN), [swap(*b) for b in beside]
    return lax.optimization_barrier(step)


def gather_z(x, dim, beside=((),) * 4):
    z = lax.axis_index("z")
    x = jnp.expand_dims(x, dim)
    shape = list(x.shape)
    shape[dim] = NZ

    def put(all_x, block, k):
        return lax.dynamic_update_slice_in_dim(all_x, block, (z + k) % NZ, dim)

    out = put(jnp.zeros(shape, x.dtype), x, 0)
    up = down = x
    swapped = []
    for k in range(1, 4):
        up, down, got = both_ways(up, down, beside[k - 1])
        swapped += got
        out = put(put(out, up, NZ - k), down, k)
    axis = 1 - dim
    half = x.shape[axis] // 2
    up = lax.slice_in_dim(up, 0, half, axis=axis)
    down = lax.slice_in_dim(down, half, 2 * half, axis=axis)
    up, down, got = both_ways(up, down, beside[3])
    return put(out, jnp.concatenate([up, down], axis=axis), 4), swapped + got


def fetch(pool, holder, slot, weights, queries):
    slots = pool.shape[0]
    z = lax.axis_index("z")
    core = lax.axis_index("core")
    queries = lax.all_to_all(queries, TP, 0, 0, tiled=True)
    mine = after(jnp.stack([holder, slot]), queries)
    theirs = swap(mine, "core")
    x = ordered(pool, swap(pool, "xlo"), "xlo").reshape(2 * slots, -1)
    ups, downs, halved = [x], [x], []
    for k in range(3):
        split = [divide(after(w, downs[k - 1]), "core", dim) for w, dim in weights[k]]
        up, down, got = both_ways(ups[-1], downs[-1], [(give, "core") for _, give in split])
        halved += [(keep, other) for (keep, _), other in zip(split, got)]
        ups.append(up)
        downs.append(down)
    *far, _ = both_ways(ups[-1][:slots], downs[-1][slots:])
    blocks = jnp.concatenate(downs + far + ups[:0:-1])
    both = jnp.concatenate([mine, theirs], axis=1)
    away = (both[0] // 2 - z) % NZ
    row = (away * 2 + both[0] // (2 * NZ)) * slots + both[1]
    row = jnp.where(both[0] % 2 == core, row, -1)
    chosen = row[:, None] == jnp.arange(blocks.shape[0], dtype=jnp.int32)[None, :]
    picked = dot(chosen.astype(BF), blocks).astype(BF)
    count = holder.shape[0]
    return picked[:count] + swap(picked[count:], "core"), halved, queries, downs[1]


def sum_tp(y):
    return jnp.sum(lax.all_to_all(y, TP, 0, 0, tiled=True).astype(F32), axis=0)


def on_device(
    queries,
    new_latent,
    hot_cache,
    cache_len,
    page_pool,
    cold_holder,
    cold_slot,
    residual,
    value_map,
    out_proj,
    norm_gain,
    gate_proj,
    up_proj,
    down_proj,
):
    shares = lax.axis_size(TP)
    share = lax.axis_index(TP)
    z = lax.axis_index("z")
    rows_dev, pages_each = cold_holder.shape
    rows_own = rows_dev // shares
    width = queries.shape[-1]
    slots = page_pool.shape[0]

    page_share = page_pool.shape[1] // shares
    pool = lax.dynamic_slice_in_dim(page_pool, share * page_share, page_share, 1)
    side = -(-width // 128) * 128
    pool = jnp.pad(pool, [(0, 0), (0, 0), (0, side - width)]).reshape(slots, -1)
    weights = [], [(gate_proj, 1), (up_proj, 1)], [(down_proj, 0), (out_proj, 0)]
    q_rows = queries.reshape(shares, rows_own, queries.shape[1], width)
    fetched, halved, q_rows, early = fetch(
        pool, cold_holder.reshape(-1), cold_slot.reshape(-1), weights, q_rows
    )
    w_gate, w_up, w_down, w_out = halved
    fetched = fetched.reshape(shares, rows_own * pages_each, -1)

    start = after(share * rows_own, early)
    hot = lax.dynamic_slice_in_dim(hot_cache, start, rows_own, 0)

    fetched, hot = lax.optimization_barrier((fetched, hot))
    cold = lax.all_to_all(fetched, TP, 0, 0, tiled=True)
    cold = cold.reshape(shares, rows_own, pages_each, -1).transpose(1, 0, 2, 3)
    cold = cold.reshape(rows_own, shares * pages_each, -1)

    lens = lax.dynamic_slice_in_dim(cache_len, start, rows_own, 0)
    new = lax.dynamic_slice_in_dim(new_latent, start, rows_own, 0)
    latent = attend(lens, q_rows, cold, hot, new)
    latent = lax.all_to_all(latent, TP, 0, 0, tiled=True)
    latent = latent.reshape(rows_dev, -1, DC)
    head_rows = jnp.einsum("bhc,hcv->bhv", latent, value_map, preferred_element_type=F32)
    head_rows = head_rows.astype(BF).reshape(rows_dev, 2, -1)

    keep = jnp.where(first("core"), head_rows[:, 0], head_rows[:, 1])
    give = jnp.where(first("core"), head_rows[:, 1], head_rows[:, 0])
    mine = ordered(keep, swap(give, "core"), "core")
    mine = ordered(mine, swap(mine, "xlo"), "xlo")

    cols, units = gate_proj.shape[0], gate_proj.shape[1] // 4
    split = [divide(after(w, mine), "xlo", 1) for w in w_gate + w_up]
    heads, got = gather_z(mine, 1, [[(give, "xlo")] for _, give in split])
    heads = heads.reshape(residual.shape[0], -1)

    row_count = residual.shape[0] // shares
    theirs = swap(dot(heads, w_out[1]).astype(BF), "core")
    partial = (dot(heads, w_out[0]) + theirs.astype(F32)).astype(BF)
    quarter = after([(keep, other) for (keep, _), other in zip(split, got)], partial)
    attended = sum_tp(partial.reshape(shares, row_count, cols))

    lanes = -(-units // 128) * 128
    deep = 256
    room = [(0, deep - cols), (0, lanes - units)]
    quarter = [jnp.pad(w, room) for pair in quarter for w in pair]
    row_id = lax.broadcasted_iota(jnp.int32, (deep, lanes), 0)
    col_id = lax.broadcasted_iota(jnp.int32, (deep, lanes), 1)
    passed = (row_id >= cols) & (row_id < cols + 2) & (col_id - units == row_id - cols)
    quarter[:4] = [jnp.where(passed, jnp.ones((), BF), w) for w in quarter[:4]]
    w_both = jnp.concatenate([jnp.concatenate(quarter[:4]), jnp.concatenate(quarter[4:])], axis=1)
    res = lax.dynamic_slice_in_dim(residual, share * row_count, row_count, 0)
    hidden = res.astype(F32) + attended

    squares = jnp.sum(hidden * hidden, axis=1, keepdims=True)
    high = squares.astype(BF)
    low = (squares - high.astype(F32)).astype(BF)
    scaled = (hidden * norm_gain.astype(F32)[None, :]).astype(BF)
    scaled = jnp.concatenate(
        [scaled, high, low, jnp.zeros((row_count, deep - cols - 2), BF)], axis=1
    )
    scaled = jnp.concatenate([scaled, swap(scaled, "xlo")], axis=1)
    scaled = jnp.broadcast_to(scaled[None], (shares,) + scaled.shape)
    scaled = lax.all_to_all(scaled, TP, 0, 0, tiled=True)
    scaled, w_both = lax.optimization_barrier((scaled, w_both))
    scaled = jnp.concatenate([scaled, swap(scaled, "core")], axis=2)

    def rows_of(x, k):
        return lax.dynamic_slice_in_dim(x, (z + k) % NZ * row_count, row_count, 0)

    scaled = scaled.reshape(shares * row_count, -1)
    split = [divide(after(w, scaled), "xlo", 0) for w in w_down]
    n = units // 2
    beside = [[(give[i : i + n], "xlo")] for _, give in split for i in (0, n)]
    far = dot(rows_of(scaled, 4), w_both).astype(BF)
    half = row_count // 2
    up, down, got = both_ways(far[:half], far[half:], beside[0])
    none = jnp.zeros_like(up)
    up = jnp.concatenate([up, none])
    down = jnp.concatenate([none, down])
    for k in (3, 2, 1):
        terms = [dot(rows_of(scaled, n), w_both).astype(BF) for n in (k, NZ - k)]
        up, down, terms = lax.optimization_barrier((up, down, terms))
        up = (terms[0].astype(F32) + up.astype(F32)).astype(BF)
        down = (terms[1].astype(F32) + down.astype(F32)).astype(BF)
        up, down, other = both_ways(up, down, beside[4 - k])
        got += other
    last = dot(rows_of(scaled, 0), w_both)
    up, down, last = lax.optimization_barrier((up, down, last))
    total = last + up.astype(F32) + down.astype(F32)
    sums = total[:, units : units + 1] + total[:, units + 1 : units + 2]
    inverse = lax.rsqrt(sums / (4 * NZ * cols) + 1e-06)
    gate = total[:, :units] * inverse
    activated = (jax.nn.silu(gate) * (total[:, lanes : lanes + units] * inverse)).astype(BF)

    activated = gather_z(activated, 0)[0].reshape(residual.shape[0], -1)
    room = [(0, 0), (0, deep - cols)]
    w_down = []
    for i in (0, 1):
        pair = ordered(split[i][0], jnp.concatenate(got[2 * i : 2 * i + 2]), "xlo")
        w_down.append(jnp.concatenate([jnp.pad(w, room) for w in pair], axis=1))
    activated, w_down = lax.optimization_barrier((activated, w_down))
    theirs = swap(dot(activated, w_down[1]).astype(BF), "core")
    partial = (dot(activated, w_down[0]) + theirs.astype(F32)).astype(BF)
    partial = jnp.stack([partial[:, :deep], partial[:, deep:]])
    partial = partial.reshape(2 * shares, row_count, deep)
    summed = lax.all_to_all(partial, ("xlo",) + TP, 0, 0, tiled=True)
    summed = jnp.sum(summed.astype(F32), axis=0)[:, :cols]
    return (hidden + summed).astype(BF)


def solution(mesh):
    grid = Mesh(mesh.devices.reshape(2, NZ, 2, 2, 4), DP + TP)
    placed = (
        P(DP, TP, None),
        P(DP, None),
        P(DP, None, None),
        P(DP),
        P(DP, None, None),
        P(DP, None),
        P(DP, None),
        P(None, DP),
        P(TP, None, None),
        P(TP, DP),
        P(DP),
        P(DP, TP),
        P(DP, TP),
        P(TP, DP),
    )
    return jax.shard_map(
        on_device, mesh=grid, in_specs=placed, out_specs=P(TP, DP), check_vma=False
    )
```

```python
import jax
import jax.numpy as jnp
from jax import lax
from jax.experimental import pallas as pl
from jax.experimental.pallas import tpu as pltpu
from jax.sharding import Mesh
from jax.sharding import PartitionSpec as P

DC = 512
DR = 64
DV = 128
NZ = 8
DP = ("xlo", "z", "core")
TP = ("xhi", "y")
BF = jnp.bfloat16
F32 = jnp.float32


def dot(a, b):
    return jnp.dot(a, b, preferred_element_type=F32)


def attend_kernel(len_ref, q_ref, cold_ref, hot_ref, new_ref, out_ref):
    scale = (DV + DR) ** (-0.5)
    heads = q_ref.shape[1] * q_ref.shape[0]
    width = q_ref.shape[-1]
    q = q_ref[...].reshape(heads, width)
    side = -(-width // 128) * 128
    cold = cold_ref[0]
    cold = [cold[:, at : at + width] for at in range(0, cold.shape[1], side)]
    cold = jnp.concatenate(cold, axis=0)
    hot = hot_ref[0]
    new = new_ref[0]
    nt = (((1,), (1,)), ((), ()))
    s_cold = lax.dot_general(q, cold, nt, preferred_element_type=F32) * scale
    s_hot = lax.dot_general(q, hot, nt, preferred_element_type=F32) * scale
    live = lax.broadcasted_iota(jnp.int32, s_hot.shape, 1) < len_ref[pl.program_id(0)]
    s_hot = jnp.where(live, s_hot, -1e30)
    s_new = jnp.sum(q.astype(F32) * new.astype(F32), axis=1, keepdims=True) * scale
    top = jnp.maximum(jnp.max(s_cold, axis=1, keepdims=True), jnp.max(s_hot, axis=1, keepdims=True))
    top = jnp.maximum(top, s_new)
    e_cold = jnp.exp(s_cold - top)
    e_hot = jnp.exp(s_hot - top)
    e_new = jnp.exp(s_new - top)
    total = jnp.sum(e_cold, axis=1, keepdims=True) + jnp.sum(e_hot, axis=1, keepdims=True) + e_new
    w_cold = (e_cold / total).astype(BF)
    w_hot = (e_hot / total).astype(BF)
    w_new = (e_new / total).astype(BF).astype(F32)
    out = dot(w_cold, cold[:, :DC]) + dot(w_hot, hot[:, :DC])
    out = out + w_new * new[:, :DC].astype(F32)
    out_ref[...] = out.astype(BF).reshape(out_ref.shape)


def attend(lens, q, cold, hot, new):
    groups, rows, heads, width = q.shape
    return pl.pallas_call(
        attend_kernel,
        grid_spec=pltpu.PrefetchScalarGridSpec(
            num_scalar_prefetch=1,
            grid=(rows,),
            in_specs=[
                pl.BlockSpec((groups, None, heads, width), lambda r, n: (0, r, 0, 0)),
                pl.BlockSpec((1,) + cold.shape[1:], lambda r, n: (r, 0, 0)),
                pl.BlockSpec((1,) + hot.shape[1:], lambda r, n: (r, 0, 0)),
                pl.BlockSpec((1, 1, width), lambda r, n: (r, 0, 0)),
            ],
            out_specs=pl.BlockSpec((groups, None, heads, DC), lambda r, n: (0, r, 0, 0)),
        ),
        out_shape=jax.ShapeDtypeStruct((groups, rows, heads, DC), BF),
        compiler_params=pltpu.CompilerParams(vmem_limit_bytes=12 << 20),
    )(lens, q, cold, hot, new[:, None, :])


UP = [(i, (i + 1) % NZ) for i in range(NZ)]
DOWN = [(i, (i - 1) % NZ) for i in range(NZ)]
SWAP = [(0, 1), (1, 0)]


def swap(x, axis):
    return lax.ppermute(x, axis, SWAP)


def first(axis):
    return lax.axis_index(axis) == 0


def ordered(mine, other, axis):
    f = first(axis)
    return jnp.stack([jnp.where(f, mine, other), jnp.where(f, other, mine)])


def divide(x, axis, dim):
    n = x.shape[dim] // 2
    low = lax.slice_in_dim(x, 0, n, axis=dim)
    high = lax.slice_in_dim(x, n, 2 * n, axis=dim)
    f = first(axis)
    return jnp.where(f, low, high), jnp.where(f, high, low)


def after(x, y):
    return lax.optimization_barrier((x, y))[0]


def both_ways(up, down, beside=()):
    beside = [(after(x, down), axis) for x, axis in beside]
    step = lax.ppermute(up, "z", UP), lax.ppermute(down, "z", DOWN), [swap(*b) for b in beside]
    return lax.optimization_barrier(step)


def gather_z(x, dim, beside=((),) * 4):
    z = lax.axis_index("z")
    x = jnp.expand_dims(x, dim)
    shape = list(x.shape)
    shape[dim] = NZ

    def put(all_x, block, k):
        return lax.dynamic_update_slice_in_dim(all_x, block, (z + k) % NZ, dim)

    out = put(jnp.zeros(shape, x.dtype), x, 0)
    up = down = x
    swapped = []
    for k in range(1, 4):
        up, down, got = both_ways(up, down, beside[k - 1])
        swapped += got
        out = put(put(out, up, NZ - k), down, k)
    axis = 1 - dim
    half = x.shape[axis] // 2
    up = lax.slice_in_dim(up, 0, half, axis=axis)
    down = lax.slice_in_dim(down, half, 2 * half, axis=axis)
    up, down, got = both_ways(up, down, beside[3])
    return put(out, jnp.concatenate([up, down], axis=axis), 4), swapped + got


def fetch(pool, holder, slot, queries):
    slots = pool.shape[0]
    z = lax.axis_index("z")
    core = lax.axis_index("core")
    x = ordered(pool, swap(pool, "xlo"), "xlo").reshape(2 * slots, -1)
    queries = lax.all_to_all(queries, TP, 0, 0, tiled=True)
    holder, slot = after((holder, slot), (queries, x))
    holder, slot = holder.reshape(-1), slot.reshape(-1)
    mine = jnp.stack([holder, slot])
    theirs = swap(mine, "core")
    ups, downs = [x], [x]
    for _ in range(3):
        up, down, _ = both_ways(ups[-1], downs[-1])
        ups.append(up)
        downs.append(down)
    *far, _ = both_ways(ups[-1][:slots], downs[-1][slots:])
    blocks = jnp.concatenate(downs + far + ups[:0:-1])
    both = jnp.concatenate([mine, theirs], axis=1)
    away = (both[0] // 2 - z) % NZ
    row = (away * 2 + both[0] // (2 * NZ)) * slots + both[1]
    row = jnp.where(both[0] % 2 == core, row, -1)
    chosen = row[:, None] == jnp.arange(blocks.shape[0], dtype=jnp.int32)[None, :]
    picked = dot(chosen.astype(BF), blocks).astype(BF)
    count = holder.shape[0]
    return picked[:count] + swap(picked[count:], "core"), queries, downs[1]


def sum_tp(y):
    return jnp.sum(lax.all_to_all(y, TP, 0, 0, tiled=True).astype(F32), axis=0)


def on_device(
    queries,
    new_latent,
    hot_cache,
    cache_len,
    page_pool,
    cold_holder,
    cold_slot,
    residual,
    value_map,
    out_proj,
    norm_gain,
    gate_proj,
    up_proj,
    down_proj,
):
    shares = lax.axis_size(TP)
    share = lax.axis_index(TP)
    z = lax.axis_index("z")
    rows_dev, pages_each = cold_holder.shape
    rows_own = rows_dev // shares
    width = queries.shape[-1]
    slots = page_pool.shape[0]

    page_share = page_pool.shape[1] // shares
    pool = lax.dynamic_slice_in_dim(page_pool, share * page_share, page_share, 1)
    side = -(-width // 128) * 128
    pool = jnp.pad(pool, [(0, 0), (0, 0), (0, side - width)]).reshape(slots, -1)
    q_rows = queries.reshape(shares, rows_own, queries.shape[1], width)
    fetched, q_rows, early = fetch(pool, cold_holder, cold_slot, q_rows)
    fetched = fetched.reshape(shares, rows_own * pages_each, -1)

    start = after(share * rows_own, early)
    hot = lax.dynamic_slice_in_dim(hot_cache, start, rows_own, 0)

    fetched, hot = lax.optimization_barrier((fetched, hot))
    weights = [(gate_proj, 1), (up_proj, 1), (down_proj, 0), (out_proj, 0)]
    split = [divide(after(w, fetched), "core", dim) for w, dim in weights]
    halved = [(keep, swap(give, "core")) for keep, give in split]
    cold = lax.all_to_all(fetched, TP, 0, 0, tiled=True)
    cold, halved = lax.optimization_barrier((cold, halved))
    w_gate, w_up, w_down, w_out = halved
    cold = cold.reshape(shares, rows_own, pages_each, -1).transpose(1, 0, 2, 3)
    cold = cold.reshape(rows_own, shares * pages_each, -1)

    lens = lax.dynamic_slice_in_dim(cache_len, start, rows_own, 0)
    new = lax.dynamic_slice_in_dim(new_latent, start, rows_own, 0)
    latent = attend(lens, q_rows, cold, hot, new)
    split = [divide(after(w, latent), "xlo", 1) for w in w_gate + w_up]
    latent = lax.all_to_all(latent, TP, 0, 0, tiled=True)
    latent, split = lax.optimization_barrier((latent, split))
    latent = latent.reshape(rows_dev, -1, DC)
    head_rows = jnp.einsum("bhc,hcv->bhv", latent, value_map, preferred_element_type=F32)
    head_rows = head_rows.astype(BF).reshape(rows_dev, 2, -1)

    keep = jnp.where(first("core"), head_rows[:, 0], head_rows[:, 1])
    give = jnp.where(first("core"), head_rows[:, 1], head_rows[:, 0])
    mine = ordered(keep, swap(give, "core"), "core")
    mine = ordered(mine, swap(mine, "xlo"), "xlo")

    cols, units = gate_proj.shape[0], gate_proj.shape[1] // 4
    heads, got = gather_z(mine, 1, [[(give, "xlo")] for _, give in split])
    heads = heads.reshape(residual.shape[0], -1)

    row_count = residual.shape[0] // shares
    theirs = swap(dot(heads, w_out[1]).astype(BF), "core")
    partial = (dot(heads, w_out[0]) + theirs.astype(F32)).astype(BF)
    quarter = after([(keep, other) for (keep, _), other in zip(split, got)], partial)
    attended = sum_tp(partial.reshape(shares, row_count, cols))

    lanes = -(-units // 128) * 128
    deep = 256
    room = [(0, deep - cols), (0, lanes - units)]
    quarter = [jnp.pad(w, room) for pair in quarter for w in pair]
    row_id = lax.broadcasted_iota(jnp.int32, (deep, lanes), 0)
    col_id = lax.broadcasted_iota(jnp.int32, (deep, lanes), 1)
    passed = (row_id >= cols) & (row_id < cols + 2) & (col_id - units == row_id - cols)
    quarter[:4] = [jnp.where(passed, jnp.ones((), BF), w) for w in quarter[:4]]
    w_both = jnp.concatenate([jnp.concatenate(quarter[:4]), jnp.concatenate(quarter[4:])], axis=1)
    res = lax.dynamic_slice_in_dim(residual, share * row_count, row_count, 0)
    hidden = res.astype(F32) + attended

    squares = jnp.sum(hidden * hidden, axis=1, keepdims=True)
    high = squares.astype(BF)
    low = (squares - high.astype(F32)).astype(BF)
    scaled = (hidden * norm_gain.astype(F32)[None, :]).astype(BF)
    scaled = jnp.concatenate(
        [scaled, high, low, jnp.zeros((row_count, deep - cols - 2), BF)], axis=1
    )
    scaled = jnp.concatenate([scaled, swap(scaled, "xlo")], axis=1)
    scaled = jnp.broadcast_to(scaled[None], (shares,) + scaled.shape)
    scaled = lax.all_to_all(scaled, TP, 0, 0, tiled=True)
    scaled, w_both = lax.optimization_barrier((scaled, w_both))
    scaled = jnp.concatenate([scaled, swap(scaled, "core")], axis=2)

    def rows_of(x, k):
        return lax.dynamic_slice_in_dim(x, (z + k) % NZ * row_count, row_count, 0)

    scaled = scaled.reshape(shares * row_count, -1)
    split = [divide(after(w, scaled), "xlo", 0) for w in w_down]
    n = units // 2
    beside = [[(give[i : i + n], "xlo")] for _, give in split for i in (0, n)]
    far = dot(rows_of(scaled, 4), w_both).astype(BF)
    half = row_count // 2
    up, down, got = both_ways(far[:half], far[half:], beside[0])
    none = jnp.zeros_like(up)
    up = jnp.concatenate([up, none])
    down = jnp.concatenate([none, down])
    x = scaled
    for k in (3, 2, 1):
        terms = [dot(rows_of(x, n), w_both).astype(BF) for n in (k, NZ - k)]
        up, down, terms = lax.optimization_barrier((up, down, terms))
        x = after(scaled, down)
        up = (terms[0].astype(F32) + up.astype(F32)).astype(BF)
        down = (terms[1].astype(F32) + down.astype(F32)).astype(BF)
        up, down, other = both_ways(up, down, beside[4 - k])
        got += other
    last = dot(rows_of(x, 0), w_both)
    up, down, last = lax.optimization_barrier((up, down, last))
    total = last + up.astype(F32) + down.astype(F32)
    sums = total[:, units : units + 1] + total[:, units + 1 : units + 2]
    inverse = lax.rsqrt(sums / (4 * NZ * cols) + 1e-06)
    gate = total[:, :units] * inverse
    activated = (jax.nn.silu(gate) * (total[:, lanes : lanes + units] * inverse)).astype(BF)

    activated = gather_z(activated, 0)[0].reshape(residual.shape[0], -1)
    room = [(0, 0), (0, deep - cols)]
    w_down = []
    for i in (0, 1):
        pair = ordered(split[i][0], jnp.concatenate(got[2 * i : 2 * i + 2]), "xlo")
        w_down.append(jnp.concatenate([jnp.pad(w, room) for w in pair], axis=1))
    activated, w_down = lax.optimization_barrier((activated, w_down))
    theirs = swap(dot(activated, w_down[1]).astype(BF), "core")
    partial = (dot(activated, w_down[0]) + theirs.astype(F32)).astype(BF)
    partial = jnp.stack([partial[:, :deep], partial[:, deep:]])
    partial = partial.reshape(2 * shares, row_count, deep)
    summed = lax.all_to_all(partial, ("xlo",) + TP, 0, 0, tiled=True)
    summed = jnp.sum(summed.astype(F32), axis=0)[:, :cols]
    return (hidden + summed).astype(BF)


def solution(mesh):
    grid = Mesh(mesh.devices.reshape(2, NZ, 2, 2, 4), DP + TP)
    placed = (
        P(DP, TP, None),
        P(DP, None),
        P(DP, None, None),
        P(DP),
        P(DP, None, None),
        P(DP, None),
        P(DP, None),
        P(None, DP),
        P(TP, None, None),
        P(TP, DP),
        P(DP),
        P(DP, TP),
        P(DP, TP),
        P(TP, DP),
    )
    return jax.shard_map(
        on_device, mesh=grid, in_specs=placed, out_specs=P(TP, DP), check_vma=False
    )
```

```python
import jax
import jax.numpy as jnp
from jax import lax
from jax.experimental import pallas as pl
from jax.experimental.pallas import tpu as pltpu
from jax.sharding import Mesh
from jax.sharding import PartitionSpec as P

DC = 512
DR = 64
DV = 128
NZ = 8
DP = ("xlo", "z", "core")
TP = ("xhi", "y")
BF = jnp.bfloat16
F32 = jnp.float32


def dot(a, b):
    return jnp.dot(a, b, preferred_element_type=F32)


def attend_kernel(len_ref, q_ref, cold_ref, hot_ref, new_ref, out_ref):
    scale = (DV + DR) ** (-0.5)
    heads = q_ref.shape[1] * q_ref.shape[0]
    width = q_ref.shape[-1]
    q = q_ref[...].reshape(heads, width)
    side = -(-width // 128) * 128
    cold = cold_ref[0]
    cold = [cold[:, at : at + width] for at in range(0, cold.shape[1], side)]
    cold = jnp.concatenate(cold, axis=0)
    hot = hot_ref[0]
    new = new_ref[0]
    nt = (((1,), (1,)), ((), ()))
    s_cold = lax.dot_general(q, cold, nt, preferred_element_type=F32) * scale
    s_hot = lax.dot_general(q, hot, nt, preferred_element_type=F32) * scale
    live = lax.broadcasted_iota(jnp.int32, s_hot.shape, 1) < len_ref[pl.program_id(0)]
    s_hot = jnp.where(live, s_hot, -1e30)
    s_new = jnp.sum(q.astype(F32) * new.astype(F32), axis=1, keepdims=True) * scale
    top = jnp.maximum(jnp.max(s_cold, axis=1, keepdims=True), jnp.max(s_hot, axis=1, keepdims=True))
    top = jnp.maximum(top, s_new)
    e_cold = jnp.exp(s_cold - top)
    e_hot = jnp.exp(s_hot - top)
    e_new = jnp.exp(s_new - top)
    total = jnp.sum(e_cold, axis=1, keepdims=True) + jnp.sum(e_hot, axis=1, keepdims=True) + e_new
    w_cold = (e_cold / total).astype(BF)
    w_hot = (e_hot / total).astype(BF)
    w_new = (e_new / total).astype(BF).astype(F32)
    out = dot(w_cold, cold[:, :DC]) + dot(w_hot, hot[:, :DC])
    out = out + w_new * new[:, :DC].astype(F32)
    out_ref[...] = out.astype(BF).reshape(out_ref.shape)


def attend(lens, q, cold, hot, new):
    groups, rows, heads, width = q.shape
    return pl.pallas_call(
        attend_kernel,
        grid_spec=pltpu.PrefetchScalarGridSpec(
            num_scalar_prefetch=1,
            grid=(rows,),
            in_specs=[
                pl.BlockSpec((groups, None, heads, width), lambda r, n: (0, r, 0, 0)),
                pl.BlockSpec((1,) + cold.shape[1:], lambda r, n: (r, 0, 0)),
                pl.BlockSpec((1,) + hot.shape[1:], lambda r, n: (r, 0, 0)),
                pl.BlockSpec((1, 1, width), lambda r, n: (r, 0, 0)),
            ],
            out_specs=pl.BlockSpec((groups, None, heads, DC), lambda r, n: (0, r, 0, 0)),
        ),
        out_shape=jax.ShapeDtypeStruct((groups, rows, heads, DC), BF),
        compiler_params=pltpu.CompilerParams(vmem_limit_bytes=12 << 20),
    )(lens, q, cold, hot, new[:, None, :])


UP = [(i, (i + 1) % NZ) for i in range(NZ)]
DOWN = [(i, (i - 1) % NZ) for i in range(NZ)]
SWAP = [(0, 1), (1, 0)]


def swap(x, axis):
    return lax.ppermute(x, axis, SWAP)


def first(axis):
    return lax.axis_index(axis) == 0


def ordered(mine, other, axis):
    f = first(axis)
    return jnp.stack([jnp.where(f, mine, other), jnp.where(f, other, mine)])


def divide(x, axis, dim):
    n = x.shape[dim] // 2
    low = lax.slice_in_dim(x, 0, n, axis=dim)
    high = lax.slice_in_dim(x, n, 2 * n, axis=dim)
    f = first(axis)
    return jnp.where(f, low, high), jnp.where(f, high, low)


def after(x, y):
    return lax.optimization_barrier((x, y))[0]


def both_ways(up, down, beside=()):
    beside = [(after(x, down), axis) for x, axis in beside]
    step = lax.ppermute(up, "z", UP), lax.ppermute(down, "z", DOWN), [swap(*b) for b in beside]
    return lax.optimization_barrier(step)


def gather_z(x, dim, beside=((),) * 4):
    z = lax.axis_index("z")
    x = jnp.expand_dims(x, dim)
    shape = list(x.shape)
    shape[dim] = NZ

    def put(all_x, block, k):
        return lax.dynamic_update_slice_in_dim(all_x, block, (z + k) % NZ, dim)

    out = put(jnp.zeros(shape, x.dtype), x, 0)
    up = down = x
    swapped = []
    for k in range(1, 4):
        up, down, got = both_ways(up, down, beside[k - 1])
        swapped += got
        out = put(put(out, up, NZ - k), down, k)
    axis = 1 - dim
    half = x.shape[axis] // 2
    up = lax.slice_in_dim(up, 0, half, axis=axis)
    down = lax.slice_in_dim(down, half, 2 * half, axis=axis)
    up, down, got = both_ways(up, down, beside[3])
    return put(out, jnp.concatenate([up, down], axis=axis), 4), swapped + got


def fetch(pool, holder, slot, queries):
    slots = pool.shape[0]
    z = lax.axis_index("z")
    core = lax.axis_index("core")
    x = ordered(pool, swap(pool, "xlo"), "xlo").reshape(2 * slots, -1)
    queries = lax.all_to_all(queries, TP, 0, 0, tiled=True)
    holder, slot = after((holder, slot), (queries, x))
    holder, slot = holder.reshape(-1), slot.reshape(-1)
    mine = jnp.stack([holder, slot])
    theirs = swap(mine, "core")
    ups, downs = [x], [x]
    for _ in range(3):
        up, down, _ = both_ways(ups[-1], downs[-1])
        ups.append(up)
        downs.append(down)
    *far, _ = both_ways(ups[-1][:slots], downs[-1][slots:])
    blocks = jnp.concatenate(downs + far + ups[:0:-1])
    both = jnp.concatenate([mine, theirs], axis=1)
    away = (both[0] // 2 - z) % NZ
    row = (away * 2 + both[0] // (2 * NZ)) * slots + both[1]
    row = jnp.where(both[0] % 2 == core, row, -1)
    chosen = row[:, None] == jnp.arange(blocks.shape[0], dtype=jnp.int32)[None, :]
    picked = dot(chosen.astype(BF), blocks).astype(BF)
    count = holder.shape[0]
    return picked[:count] + swap(picked[count:], "core"), queries, downs[1]


def sum_tp(y):
    return jnp.sum(lax.all_to_all(y, TP, 0, 0, tiled=True).astype(F32), axis=0)


def on_device(
    queries,
    new_latent,
    hot_cache,
    cache_len,
    page_pool,
    cold_holder,
    cold_slot,
    residual,
    value_map,
    out_proj,
    norm_gain,
    gate_proj,
    up_proj,
    down_proj,
):
    shares = lax.axis_size(TP)
    share = lax.axis_index(TP)
    z = lax.axis_index("z")
    rows_dev, pages_each = cold_holder.shape
    rows_own = rows_dev // shares
    width = queries.shape[-1]
    slots = page_pool.shape[0]

    page_share = page_pool.shape[1] // shares
    pool = lax.dynamic_slice_in_dim(page_pool, share * page_share, page_share, 1)
    side = -(-width // 128) * 128
    pool = jnp.pad(pool, [(0, 0), (0, 0), (0, side - width)]).reshape(slots, -1)
    q_rows = queries.reshape(shares, rows_own, queries.shape[1], width)
    fetched, q_rows, early = fetch(pool, cold_holder, cold_slot, q_rows)
    fetched = fetched.reshape(shares, rows_own * pages_each, -1)

    start = after(share * rows_own, early)
    hot = lax.dynamic_slice_in_dim(hot_cache, start, rows_own, 0)

    fetched, hot = lax.optimization_barrier((fetched, hot))
    weights = [(gate_proj, 1), (up_proj, 1), (down_proj, 0), (out_proj, 0)]
    split = [divide(after(w, fetched), "core", dim) for w, dim in weights]
    halved = [(keep, swap(give, "core")) for keep, give in split]
    cold = lax.all_to_all(fetched, TP, 0, 0, tiled=True)
    cold, halved = lax.optimization_barrier((cold, halved))
    w_gate, w_up, w_down, w_out = halved
    cold = cold.reshape(shares, rows_own, pages_each, -1).transpose(1, 0, 2, 3)
    cold = cold.reshape(rows_own, shares * pages_each, -1)

    lens = lax.dynamic_slice_in_dim(cache_len, start, rows_own, 0)
    new = lax.dynamic_slice_in_dim(new_latent, start, rows_own, 0)
    latent = attend(lens, q_rows, cold, hot, new)
    split = [divide(after(w, latent), "xlo", 1) for w in w_gate + w_up]
    latent = lax.all_to_all(latent, TP, 0, 0, tiled=True)
    latent, split = lax.optimization_barrier((latent, split))
    latent = latent.reshape(rows_dev, -1, DC)
    head_rows = jnp.einsum("bhc,hcv->bhv", latent, value_map, preferred_element_type=F32)
    head_rows = head_rows.astype(BF).reshape(rows_dev, 2, -1)

    keep = jnp.where(first("core"), head_rows[:, 0], head_rows[:, 1])
    give = jnp.where(first("core"), head_rows[:, 1], head_rows[:, 0])
    mine = ordered(keep, swap(give, "core"), "core")
    mine = ordered(mine, swap(mine, "xlo"), "xlo")

    cols, units = gate_proj.shape[0], gate_proj.shape[1] // 4
    heads, got = gather_z(mine, 1, [[(give, "xlo")] for _, give in split])
    heads = heads.reshape(residual.shape[0], -1)

    row_count = residual.shape[0] // shares
    theirs = swap(dot(heads, w_out[1]).astype(BF), "core")
    partial = (dot(heads, w_out[0]) + theirs.astype(F32)).astype(BF)
    quarter = after([(keep, other) for (keep, _), other in zip(split, got)], partial)
    attended = sum_tp(partial.reshape(shares, row_count, cols))

    lanes = -(-units // 128) * 128
    deep = 256
    room = [(0, deep - cols), (0, lanes - units)]
    quarter = [jnp.pad(w, room) for pair in quarter for w in pair]
    row_id = lax.broadcasted_iota(jnp.int32, (deep, lanes), 0)
    col_id = lax.broadcasted_iota(jnp.int32, (deep, lanes), 1)
    passed = (row_id >= cols) & (row_id < cols + 2) & (col_id - units == row_id - cols)
    quarter[:4] = [jnp.where(passed, jnp.ones((), BF), w) for w in quarter[:4]]
    w_both = jnp.concatenate([jnp.concatenate(quarter[:4]), jnp.concatenate(quarter[4:])], axis=1)
    res = lax.dynamic_slice_in_dim(residual, share * row_count, row_count, 0)
    hidden = res.astype(F32) + attended

    squares = jnp.sum(hidden * hidden, axis=1, keepdims=True)
    high = squares.astype(BF)
    low = (squares - high.astype(F32)).astype(BF)
    scaled = (hidden * norm_gain.astype(F32)[None, :]).astype(BF)
    scaled = jnp.concatenate(
        [scaled, high, low, jnp.zeros((row_count, deep - cols - 2), BF)], axis=1
    )
    scaled = jnp.concatenate([scaled, swap(scaled, "xlo")], axis=1)
    scaled = jnp.broadcast_to(scaled[None], (shares,) + scaled.shape)
    scaled = lax.all_to_all(scaled, TP, 0, 0, tiled=True)
    scaled, w_both = lax.optimization_barrier((scaled, w_both))
    pieces = scaled, swap(scaled, "core")
    scaled = jnp.concatenate(pieces, axis=2)

    def rows_of(x, k):
        return lax.dynamic_slice_in_dim(x, (z + k) % NZ * row_count, row_count, 0)

    scaled = scaled.reshape(shares * row_count, -1)
    split = [divide(after(w, scaled), "xlo", 0) for w in w_down]
    n = units // 2
    beside = [[(give[i : i + n], "xlo")] for _, give in split for i in (0, n)]
    pieces = [p.reshape(shares * row_count, -1) for p in pieces]
    far = dot(rows_of(pieces[0], 4), w_both[: 2 * deep])
    far = (far + dot(rows_of(pieces[1], 4), w_both[2 * deep :])).astype(BF)
    half = row_count // 2
    up, down, got = both_ways(far[:half], far[half:], beside[0])
    none = jnp.zeros_like(up)
    up = jnp.concatenate([up, none])
    down = jnp.concatenate([none, down])
    x = scaled
    for k in (3, 2, 1):
        terms = [dot(rows_of(x, n), w_both).astype(BF) for n in (k, NZ - k)]
        up, down, terms = lax.optimization_barrier((up, down, terms))
        x = after(scaled, down)
        up = (terms[0].astype(F32) + up.astype(F32)).astype(BF)
        down = (terms[1].astype(F32) + down.astype(F32)).astype(BF)
        up, down, other = both_ways(up, down, beside[4 - k])
        got += other
    last = dot(rows_of(x, 0), w_both)
    up, down, last = lax.optimization_barrier((up, down, last))
    total = last + up.astype(F32) + down.astype(F32)
    sums = total[:, units : units + 1] + total[:, units + 1 : units + 2]
    inverse = lax.rsqrt(sums / (4 * NZ * cols) + 1e-06)
    gate = total[:, :units] * inverse
    activated = (jax.nn.silu(gate) * (total[:, lanes : lanes + units] * inverse)).astype(BF)

    activated = gather_z(activated, 0)[0].reshape(residual.shape[0], -1)
    room = [(0, 0), (0, deep - cols)]
    w_down = []
    for i in (0, 1):
        pair = ordered(split[i][0], jnp.concatenate(got[2 * i : 2 * i + 2]), "xlo")
        w_down.append(jnp.concatenate([jnp.pad(w, room) for w in pair], axis=1))
    activated, w_down = lax.optimization_barrier((activated, w_down))
    theirs = swap(dot(activated, w_down[1]).astype(BF), "core")
    partial = (dot(activated, w_down[0]) + theirs.astype(F32)).astype(BF)
    partial = jnp.stack([partial[:, :deep], partial[:, deep:]])
    partial = partial.reshape(2 * shares, row_count, deep)
    summed = lax.all_to_all(partial, ("xlo",) + TP, 0, 0, tiled=True)
    summed = jnp.sum(summed.astype(F32), axis=0)[:, :cols]
    return (hidden + summed).astype(BF)


def solution(mesh):
    grid = Mesh(mesh.devices.reshape(2, NZ, 2, 2, 4), DP + TP)
    placed = (
        P(DP, TP, None),
        P(DP, None),
        P(DP, None, None),
        P(DP),
        P(DP, None, None),
        P(DP, None),
        P(DP, None),
        P(None, DP),
        P(TP, None, None),
        P(TP, DP),
        P(DP),
        P(DP, TP),
        P(DP, TP),
        P(TP, DP),
    )
    return jax.shard_map(
        on_device, mesh=grid, in_specs=placed, out_specs=P(TP, DP), check_vma=False
    )
```
